32 devices in a mesh: dp: 4 (over y, x), tensor: 8 (over z, core).
Axes of the slice: x: 2, y: 2, z: 4, core: 2. Of those that a mesh axis runs over, the one named last changes fastest.
Arguments:
- tokens: bfloat16 [8, 1024, 1024], P(None, 'dp'), may hold values from -6 to 6
- cotangent: bfloat16 [8, 1024, 1024], P(None, 'dp'), may hold values from -6 to 6
- lengths: int32 [8], replicated, may hold values from 256 to 1024, as said below
- seq_deal: int32 [8], replicated, may hold values from 0 to 7, as said below
- norm_gains: bfloat16 [2, 2, 1024], replicated, may hold values from 0.5 to 1.5
- norm_shifts: bfloat16 [2, 2, 1024], replicated, may hold values from -2 to 2
- qkv_weight: bfloat16 [2, 1024, 3072], P(None, None, 'tensor'), may hold values from -0.1875 to 0.1875
- qkv_bias: bfloat16 [2, 3072], P(None, 'tensor'), may hold values from -2 to 2
- out_weight: bfloat16 [2, 1024, 1024], P(None, 'tensor'), may hold values from -0.5 to 0.5
- proj_bias: bfloat16 [2, 2, 1024], replicated, may hold values from -2 to 2
- up_weight: bfloat16 [2, 1024, 4096], P(None, None, 'tensor'), may hold values from -0.1875 to 0.1875
- up_bias: bfloat16 [2, 4096], P(None, 'tensor'), may hold values from -2 to 2
- down_weight: bfloat16 [2, 4096, 1024], P(None, 'tensor'), may hold values from -0.09375 to 0.09375
Outputs:
- activations: bfloat16 [8, 4, 256, 1024], P('dp', None, 'tensor')
- input_grad: bfloat16 [8, 1024, 1024], P(None, 'dp')
- grad_gains: float32 [2, 2, 1024], replicated
- grad_shifts: float32 [2, 2, 1024], replicated
- grad_qkv_weight: float32 [2, 1024, 3072], P(None, None, 'tensor')
- grad_qkv_bias: float32 [2, 3072], P(None, 'tensor')
- grad_out_weight: float32 [2, 1024, 1024], P(None, 'tensor')
- grad_proj_bias: float32 [2, 2, 1024], replicated
- grad_up_weight: float32 [2, 1024, 4096], P(None, None, 'tensor')
- grad_up_bias: float32 [2, 4096], P(None, 'tensor')
- grad_down_weight: float32 [2, 4096, 1024], P(None, 'tensor')
The draws below stay inside these ranges and needn't reach their ends.
Inputs may be any that keep to these rules, and one draw needn't show every extreme that they name: `lengths`: at least one sequence has exactly 1024 tokens. `seq_deal`: A permutation of the sequence numbers; slots m = j * 2 to (j + 1) * 2 - 1 belong to index j of dp.
All inputs are finite; a program needn't handle non-finite values.
Results may differ from the reference program's by a relative error of at most 0.028.
Values may be sent and summed in bfloat16 or wider, within the bound.
No kernel may reach another device: no remote copies, remote signals or barrier semaphores. Data moves between devices by JAX's collectives and lax.ppermute only.
A program may use at most 192 MiB of HBM per device.

```python
import math
import jax
import jax.numpy as jnp
from jax import lax

D = 1024
HEADS = 16
FF = 4096
LAYERS = 2
MAXLEN = 1024
SEQ_DEV = 2
MINLEN = 256
NSEQ = 8
POS_DEV = 256


def seq_lengths(key):
    key = jax.random.fold_in(key, 11)
    pick_key, base_key = jax.random.split(key)
    drawn = jax.random.randint(base_key, (NSEQ,), MINLEN, MAXLEN + 1)
    longest = jax.random.randint(pick_key, (), 0, NSEQ)
    return jnp.where(jnp.arange(NSEQ) == longest, MAXLEN, drawn).astype(jnp.int32)


def draw_lengths(key, part):
    return seq_lengths(key)


def draw_seq_deal(key, part):
    lengths = seq_lengths(key)
    key = jax.random.fold_in(key, 5)
    tie_key, shard_key = jax.random.split(key)
    shard_count = NSEQ // SEQ_DEV
    ties = jax.random.permutation(tie_key, NSEQ).astype(jnp.int32)
    order = jnp.argsort(-(lengths * NSEQ + ties)).astype(jnp.int32)
    ranks = jnp.arange(NSEQ)
    rounds = ranks // shard_count
    within = ranks % shard_count
    shards = jnp.where(rounds % 2 == 0, within, shard_count - 1 - within)
    shards = jax.random.permutation(shard_key, shard_count)[shards]
    return jnp.zeros((NSEQ,), jnp.int32).at[shards * SEQ_DEV + rounds].set(order)


def block_levels(key, dims, cuts, smallest, high):
    def one(axis_at, parts):
        heights = jax.random.uniform(jax.random.fold_in(jax.random.fold_in(key, 6), axis_at), (parts,), jnp.float32, smallest / len(cuts), high / len(cuts))
        return jnp.repeat(jnp.exp(heights), dims[axis_at] // parts).reshape((-1,) + (1,) * (len(dims) - axis_at - 1))

    level = one(*cuts[0])
    for cut in cuts[1:]:
        level = level * one(*cut)
    return level


def normal_values(own_key, dims, spread, limit, cuts=(), held_as=jnp.bfloat16):
    array = spread * jax.random.normal(own_key, dims, jnp.float32)
    if cuts:
        array = array * block_levels(own_key, dims, cuts, -0.22, 0.18)
    return jnp.clip(array, -limit, limit).astype(held_as)


def setup_inputs(seed: int = 0) -> dict:
    seeds = jax.random.split(jax.random.key(seed), 14)
    tokens = normal_values(seeds[0], (NSEQ, MAXLEN, D), 1.0, 6.0, ((1, 4),))
    cotangent = normal_values(seeds[1], (NSEQ, MAXLEN, D), 1.0, 6.0, ((1, 4),))
    lengths = draw_lengths(jax.random.fold_in(seeds[13], 71), 0)
    seq_deal = draw_seq_deal(jax.random.fold_in(seeds[13], 71), 0)
    norm_gains = jnp.clip(1.0 + 0.1 * jax.random.normal(seeds[4], (LAYERS, 2, D), jnp.float32), 0.5, 1.5).astype(jnp.bfloat16)
    norm_shifts = normal_values(seeds[5], (LAYERS, 2, D), 0.3, 2.0)
    qkv_weight = normal_values(seeds[6], (LAYERS, D, 3 * D), D ** -0.5, 0.1875, ((2, 8),))
    qkv_bias = normal_values(seeds[7], (LAYERS, 3 * D), 0.3, 2.0, ((1, 8),))
    out_weight = normal_values(seeds[8], (LAYERS, D, D), (D // 8) ** -0.5, 0.5, ((1, 8),))
    proj_bias = normal_values(seeds[9], (LAYERS, 2, D), 0.3, 2.0)
    up_weight = normal_values(seeds[10], (LAYERS, D, FF), D ** -0.5, 0.1875, ((2, 8),))
    up_bias = normal_values(seeds[11], (LAYERS, FF), 0.3, 2.0, ((1, 8),))
    down_weight = normal_values(seeds[12], (LAYERS, FF, D), FF ** -0.5, 0.09375, ((1, 8),))
    return {"tokens": tokens, "cotangent": cotangent, "lengths": lengths, "seq_deal": seq_deal, "norm_gains": norm_gains, "norm_shifts": norm_shifts, "qkv_weight": qkv_weight, "qkv_bias": qkv_bias, "out_weight": out_weight, "proj_bias": proj_bias, "up_weight": up_weight, "up_bias": up_bias, "down_weight": down_weight}


@jax.custom_vjp
def low(v):
    return lax.optimization_barrier(v.astype(jnp.bfloat16)).astype(jnp.float32)

@jax.custom_vjp
def low_back(v):
    return v

def low_keep(v):
    return (low(v), None)

def low_pass(kept, grad):
    return (grad,)

def back_keep(v):
    return (v, None)

def back_low(kept, grad):
    return (low(grad),)
low.defvjp(low_keep, low_pass)
low_back.defvjp(back_keep, back_low)
epsilon = 1e-05

def product(left_side, right_side):
    return jnp.dot(left_side, right_side, precision=lax.Precision.HIGHEST, preferred_element_type=jnp.float32)

def layer_norm(values, gain_row, shift_row):
    center = values - lax.optimization_barrier(jnp.mean(values, -1, keepdims=True))
    variance = lax.optimization_barrier(jnp.mean(center * center, -1, keepdims=True))
    return center * lax.rsqrt(variance + epsilon) * gain_row + shift_row

def attend_sequence(packed):
    queries, key_rows, values, length = packed
    seq_len = queries.shape[0]
    scaling = queries.shape[2] ** (-0.5)
    row_index = jnp.arange(seq_len)[:, None]
    col_index = jnp.arange(seq_len)[None, :]
    slopes = jnp.exp2(-8.0 * (jnp.arange(HEADS) + 1).astype(jnp.float32) / HEADS)
    scores = jnp.einsum('qhd,khd->hqk', queries, key_rows, precision=lax.Precision.HIGHEST) * scaling
    scores = low_back(scores + slopes[:, None, None] * (col_index - row_index).astype(jnp.float32))
    allowed = (col_index <= row_index) & (col_index < length)
    weights = jax.nn.softmax(jnp.where(allowed[None], scores, -1e+30), axis=-1)
    return jnp.einsum('hqk,khd->qhd', low(weights), values, precision=lax.Precision.HIGHEST)

def forward(params, tokens, lengths):
    norm_gains, norm_shifts, qkv_weight, qkv_bias, out_weight, proj_bias, up_weight, up_bias, down_weight = params
    seq_count, seq_len, features = tokens.shape
    head_dim = features // HEADS
    pad_mask = (jnp.arange(seq_len)[None, :] < lengths[:, None]).astype(jnp.float32)[:, :, None]
    residual = (tokens * pad_mask).reshape(seq_count * seq_len, features)
    for layer_index in range(LAYERS):
        normed = low(layer_norm(residual, norm_gains[layer_index, 0], norm_shifts[layer_index, 0]))
        mixed_rows = low(low_back(product(normed, qkv_weight[layer_index]) + qkv_bias[layer_index]))
        mixed_rows = mixed_rows.reshape(seq_count, seq_len, HEADS, 3, head_dim)
        context = lax.map(jax.checkpoint(attend_sequence), (mixed_rows[:, :, :, 0], mixed_rows[:, :, :, 1], mixed_rows[:, :, :, 2], lengths))
        context = low(low_back(context.reshape(seq_count * seq_len, features)))
        residual = residual + low_back(product(context, out_weight[layer_index]) + proj_bias[layer_index, 0])
        normed = low(layer_norm(residual, norm_gains[layer_index, 1], norm_shifts[layer_index, 1]))
        upward = low_back(product(normed, up_weight[layer_index]) + up_bias[layer_index])
        activated = low(jax.nn.gelu(upward, approximate=True))
        residual = residual + low_back(product(activated, down_weight[layer_index]) + proj_bias[layer_index, 1])
    return residual.reshape(seq_count, seq_len, features) * pad_mask

def reference(tokens, cotangent, lengths, seq_deal, norm_gains, norm_shifts, qkv_weight, qkv_bias, out_weight, proj_bias, up_weight, up_bias, down_weight):
    params = tuple((argument.astype(jnp.float32) for argument in (norm_gains, norm_shifts, qkv_weight, qkv_bias, out_weight, proj_bias, up_weight, up_bias, down_weight)))
    group_size = math.gcd(NSEQ, max(1, 4096 // MAXLEN))
    group_count = NSEQ // group_size

    def shaped(argument):
        return argument.reshape((group_count, group_size) + argument.shape[1:])

    def one_group(totals, packed):
        group_tokens, group_cot, group_lengths = packed
        outputs, pull_back = jax.vjp(lambda weights, inputs: forward(weights, inputs, group_lengths), params, group_tokens.astype(jnp.float32))
        weight_grads, input_grads = pull_back(group_cot.astype(jnp.float32))
        return (jax.tree.map(jnp.add, totals, weight_grads), (outputs, input_grads))
    empty_grads = tuple((jnp.zeros(argument.shape, jnp.float32) for argument in params))
    totals, (outputs, input_grads) = lax.scan(one_group, empty_grads, (shaped(tokens), shaped(cotangent), shaped(lengths)))
    outputs = outputs.reshape(NSEQ, MAXLEN, D)
    dealt = jnp.take(outputs, seq_deal, axis=0).reshape(NSEQ, NSEQ // SEQ_DEV, POS_DEV, D)
    return (dealt.astype(jnp.bfloat16), input_grads.reshape(NSEQ, MAXLEN, D).astype(jnp.bfloat16), totals[0], totals[1], totals[2], totals[3], totals[4], totals[5], totals[6], totals[7], totals[8])
```

```python
import math

import jax
import jax.numpy as jnp
from jax import lax
from jax.sharding import PartitionSpec as P

HEADS = 16
LAYERS = 2
EPSILON = 1e-05
BF16 = jnp.bfloat16
F32 = jnp.float32


def dot(left_side, right_side, left_dim, right_dim):
    return lax.dot_general(
        left_side,
        right_side,
        (((left_dim,), (right_dim,)), ((), ())),
        preferred_element_type=F32,
    )


def norm_parts(values):
    center = values - jnp.mean(values, -1, keepdims=True)
    variance = jnp.mean(center * center, -1, keepdims=True)
    return center, lax.rsqrt(variance + EPSILON)


def layer_norm(values, gain_row, shift_row):
    center, inverse = norm_parts(values)
    return center * inverse * gain_row + shift_row


def norm_back(values, gain_row, norm_grad):
    center, inverse = norm_parts(values)
    unit = center * inverse
    scaled = norm_grad * gain_row
    gain_grad = jnp.sum(norm_grad * unit, 0)
    shift_grad = jnp.sum(norm_grad, 0)
    through = inverse * (
        scaled
        - jnp.mean(scaled, -1, keepdims=True)
        - unit * jnp.mean(scaled * unit, -1, keepdims=True)
    )
    return through, gain_grad, shift_grad


def gelu_pair(values):
    root = math.sqrt(2.0 / math.pi)
    square = values * values
    bend = jnp.tanh(root * values * (1.0 + 0.044715 * square))
    half = 0.5 * (1.0 + bend)
    slope = half + 0.5 * values * (1.0 - bend * bend) * root * (1.0 + 3 * 0.044715 * square)
    return values * half, slope


def score_table(queries, key_rows, slopes, position, length):
    scaling = queries.shape[2] ** (-0.5)
    scores = jnp.einsum("qhd,khd->hqk", queries, key_rows, preferred_element_type=F32) * scaling
    offset = (position[None, :] - position[:, None]).astype(F32)
    scores = scores + slopes[:, None, None] * offset
    allowed = (position[None, :] <= position[:, None]) & (position[None, :] < length)
    return jnp.where(allowed[None], scores, -1e30)


def attend_forward(queries, key_rows, values, slopes, position, length):
    scores = score_table(queries, key_rows, slopes, position, length)
    highest = jnp.max(scores, -1, keepdims=True)
    log_total = highest + jnp.log(jnp.sum(jnp.exp(scores - highest), -1, keepdims=True))
    weights = jnp.exp(scores - log_total).astype(BF16)
    context = jnp.einsum("hqk,khd->qhd", weights, values, preferred_element_type=F32)
    return context.astype(BF16), log_total


def attend_backward(queries, key_rows, values, slopes, position, length, log_total, context_grad):
    scaling = queries.shape[2] ** (-0.5)
    weights = jnp.exp(score_table(queries, key_rows, slopes, position, length) - log_total)
    weight_grad = jnp.einsum("qhd,khd->hqk", context_grad, values, preferred_element_type=F32)
    value_grad = jnp.einsum(
        "hqk,qhd->khd", weights.astype(BF16), context_grad, preferred_element_type=F32
    )
    center = jnp.sum(weight_grad * weights, -1, keepdims=True)
    score_grad = (weights * (weight_grad - center)).astype(BF16)
    query_grad = (
        jnp.einsum("hqk,khd->qhd", score_grad, key_rows, preferred_element_type=F32) * scaling
    )
    key_grad = (
        jnp.einsum("hqk,qhd->khd", score_grad, queries, preferred_element_type=F32) * scaling
    )
    return jnp.stack([query_grad, key_grad, value_grad], 1).astype(BF16)


def make_body(data_size, tensor_size):
    X = math.isqrt(data_size)
    Y = data_size // X
    C = 2
    Z = tensor_size // C
    OWN = Z // X

    def send(value, rule):
        pairs = []
        for y in range(Y):
            for x in range(X):
                for z in range(Z):
                    for c in range(C):
                        target = rule(y, x, z, c)
                        if target is not None:
                            ty, tx, tz, tc = target
                            pairs.append(
                                (
                                    ((y * X + x) * Z + z) * C + c,
                                    ((ty * X + tx) * Z + tz) * C + tc,
                                )
                            )
        return lax.ppermute(value, ("dp", "tensor"), pairs)

    def body(
        tokens,
        cotangent,
        lengths,
        seq_deal,
        norm_gains,
        norm_shifts,
        qkv_weight,
        qkv_bias,
        out_weight,
        proj_bias,
        up_weight,
        up_bias,
        down_weight,
    ):
        data_rank = lax.axis_index("dp")
        tensor_rank = lax.axis_index("tensor")
        y_at, x_at = data_rank // X, data_rank % X
        z_at, c_at = tensor_rank // C, tensor_rank % C
        seq_total, held_len, features = tokens.shape
        head_dim = features // HEADS
        group = X * C
        blocks = Y // C
        rows_here = blocks * held_len
        seq_len = rows_here * group
        is_owner = z_at // OWN == x_at

        def spread(rows):
            near = [rows] + [send(rows, lambda y, x, z, c: (y, x, z, (c + 1) % C))]
            pieces = list(near)
            for step in range(1, X):
                got = send(rows, lambda y, x, z, c: (y, (x - step) % X, z, c))
                pieces += [got, send(got, lambda y, x, z, c: (y, x, z, (c + 1) % C))]
            return jnp.concatenate(pieces, 0)

        def collect(left_side, weight, weight_dim):
            half_rows = C * rows_here
            total = None
            for step in list(range(1, X)) + [0]:
                part = dot(
                    left_side[step * half_rows : (step + 1) * half_rows], weight, 1, weight_dim
                ).astype(BF16)
                got = send(part[rows_here:], lambda y, x, z, c: (y, x, z, (c + 1) % C))
                part = part[:rows_here].astype(F32) + got.astype(F32)
                if step:
                    part = send(
                        part.astype(BF16), lambda y, x, z, c: (y, (x + step) % X, z, c)
                    ).astype(F32)
                total = part if total is None else total + part
            return total

        def fetch(piece):
            arrived = None
            for step in range(1, Z // OWN):
                got = send(
                    piece,
                    lambda y, x, z, c: (
                        (y, x, (z + OWN * step) % Z, c) if z // OWN == x else None
                    ),
                )
                arrived = got if arrived is None else arrived + got
            piece = jnp.where(is_owner, piece, arrived)
            shards = [piece] + [
                send(piece, lambda y, x, z, c: (y, x, z // OWN * OWN + (z - step) % OWN, c))
                for step in range(1, OWN)
            ]
            full = []
            for shard in shards:
                full.append(shard)
                for step in range(1, Y):
                    full.append(send(shard, lambda y, x, z, c: ((y - step) % Y, x, z, c)))
            return full

        def settle(parts, wire=BF16):
            sums = []
            for shard in range(OWN):
                here = parts[shard * Y].astype(F32)
                for step in range(1, Y):
                    here += send(
                        parts[shard * Y + step].astype(wire),
                        lambda y, x, z, c: ((y + step) % Y, x, z, c),
                    ).astype(F32)
                sums.append(here)
            here = sums[0]
            for step in range(1, OWN):
                here += send(
                    sums[step].astype(wire),
                    lambda y, x, z, c: (y, x, z // OWN * OWN + (z + step) % OWN, c),
                ).astype(F32)
            low = here.astype(wire)
            for step in range(1, Z // OWN):
                here += send(
                    low,
                    lambda y, x, z, c: (
                        (y, x, (z + OWN * step) % Z, c)
                        if ((z + OWN * step) % Z) // OWN == x
                        else None
                    ),
                ).astype(F32)
            low = here.astype(wire)
            arrived = None
            for step in range(1, X):
                got = send(
                    low,
                    lambda y, x, z, c: ((y, (x + step) % X, z, c) if z // OWN == x else None),
                )
                arrived = got if arrived is None else arrived + got
            low = jnp.where(is_owner, low, arrived)
            relative = [low] + [
                send(low, lambda y, x, z, c: ((y - step) % Y, x, z, c)) for step in range(1, Y)
            ]
            stacked = jnp.stack(relative)
            return jnp.roll(stacked, y_at, 0) if Y > 2 else jnp.where(
                y_at == 0, stacked, stacked[::-1]
            )

        def own_part(array, axis):
            size = array.shape[axis] // Y
            return lax.dynamic_slice_in_dim(array, y_at * size, size, axis)

        shard_heads = qkv_weight.shape[2] // (3 * head_dim)
        shard_width = shard_heads * head_dim
        weights = []
        bias_rows = []
        qkv_bias_view = (
            qkv_bias.reshape(LAYERS, shard_heads, 3, head_dim)
            .transpose(0, 2, 1, 3)
            .reshape(LAYERS, 3, shard_width)
        )
        qkv_bias_part = own_part(qkv_bias_view, 2).reshape(1, -1)
        up_bias_part = own_part(up_bias, 1).reshape(1, -1)
        bias_cut = qkv_bias_part.shape[1]
        bias_parts = fetch(jnp.concatenate([qkv_bias_part, up_bias_part], 1))
        full_qkv_bias = jnp.concatenate(
            [part[0, :bias_cut].reshape(LAYERS, 3, -1) for part in bias_parts], 2
        ).reshape(LAYERS, -1).astype(F32)
        full_up_bias = jnp.concatenate(
            [part[0, bias_cut:].reshape(LAYERS, -1) for part in bias_parts], 1
        ).astype(F32)
        for layer in range(LAYERS):
            qkv_view = (
                qkv_weight[layer]
                .reshape(features, shard_heads, 3, head_dim)
                .transpose(2, 1, 3, 0)
                .reshape(3, shard_width, features)
            )
            qkv_full = jnp.concatenate(fetch(own_part(qkv_view, 1)), 1).reshape(-1, features)
            out_full = jnp.concatenate(fetch(own_part(out_weight[layer], 0)), 0)
            up_full = jnp.concatenate(fetch(own_part(up_weight[layer], 1)), 1)
            down_full = jnp.concatenate(fetch(own_part(down_weight[layer], 0)), 0)
            weights.append((qkv_full, out_full, up_full, down_full))

        head_here = weights[0][1].shape[0] // head_dim
        part_width = shard_width // Y
        element = jnp.arange(head_here) * head_dim
        shard_step = element // shard_width
        y_step = element % shard_width // part_width
        shard_z = x_at * OWN + (z_at + shard_step) % OWN
        y_true = (y_at + y_step) % Y
        head_ids = ((shard_z * C + c_at) * shard_width + y_true * part_width) // head_dim
        slopes = jnp.exp2(-8.0 * (head_ids + 1).astype(F32) / HEADS)

        slot = y_at * Z + z_at
        sequence = seq_deal[slot]
        length = lengths[sequence]

        def deal(member):
            pieces = []
            for step in range(Y):
                target = (y_at + step) % Y
                picked = lax.dynamic_index_in_dim(
                    member, seq_deal[target * Z + z_at], 0, keepdims=False
                )
                if step:
                    picked = send(
                        picked,
                        lambda y, x, z, c: (
                            ((y + step) % Y, x, z, c) if y // blocks == c else None
                        ),
                    )
                pieces.append(picked)
            if Y == 2:
                return jnp.where(y_at == c_at, pieces[0], pieces[1])
            stacked = jnp.stack(pieces)
            wanted = (y_at - (c_at * blocks + jnp.arange(blocks))) % Y
            return jnp.take(stacked, wanted, axis=0).reshape(-1, features)

        def positions(x_of, c_of):
            block = (c_of * blocks + jnp.arange(blocks)) * X + x_of
            return (block[:, None] * held_len + jnp.arange(held_len)[None, :]).reshape(-1)

        own_position = positions(x_at, c_at)
        position = jnp.concatenate(
            [
                positions((x_at + x_step) % X, (c_at + c_step) % C)
                for x_step in range(X)
                for c_step in range(C)
            ]
        )
        keep_rows = (own_position < length).astype(F32)[:, None]
        residual = deal(tokens).astype(F32) * keep_rows
        grad_rows = deal(cotangent).astype(F32) * keep_rows

        def split_heads(rows):
            cut = rows.reshape(seq_len, 3, head_here, head_dim)
            return cut[:, 0], cut[:, 1], cut[:, 2]

        saved = []
        for layer in range(LAYERS):
            qkv_full, out_full, up_full, down_full = weights[layer]
            gains = norm_gains[layer].astype(F32)
            shifts = norm_shifts[layer].astype(F32)
            biases = proj_bias[layer].astype(F32)
            before = residual
            first_norm = spread(layer_norm(before, gains[0], shifts[0]).astype(BF16))
            mixed = (dot(first_norm, qkv_full, 1, 1) + full_qkv_bias[layer]).astype(BF16)
            context, log_total = attend_forward(*split_heads(mixed), slopes, position, length)
            context = context.reshape(seq_len, -1)
            middle = before + (collect(context, out_full, 0) + biases[0])
            second_norm = spread(layer_norm(middle, gains[1], shifts[1]).astype(BF16))
            upward = dot(second_norm, up_full, 1, 0) + full_up_bias[layer]
            activated, act_slope = gelu_pair(upward)
            activated = activated.astype(BF16)
            act_slope = act_slope.astype(BF16)
            residual = middle + (collect(activated, down_full, 0) + biases[1])
            saved.append(
                (
                    before,
                    first_norm,
                    mixed,
                    log_total,
                    context,
                    middle,
                    second_norm,
                    activated,
                    act_slope,
                )
            )

        final = (residual * keep_rows).astype(BF16)
        slots_dev = seq_total // (Y * X)
        moved = []
        for step in range(X):
            source = final
            if step:
                source = send(
                    final,
                    lambda y, x, z, c: (
                        (y, (x + step) % X, z, c) if (x + step) % X == z // slots_dev else None
                    ),
                )
            moved.append(source)
        moved = jnp.stack(moved)
        order = (x_at - jnp.arange(X)) % X
        moved = jnp.take(moved, order, axis=0)
        share = held_len // tensor_size
        moved = moved.reshape(X, blocks, Z, C, share, features)
        by_z = []
        for step in range(Z):
            outgoing = lax.dynamic_index_in_dim(moved, (z_at + step) % Z, 2, keepdims=False)
            if step:
                outgoing = send(
                    outgoing,
                    lambda y, x, z, c: (
                        (y, x, (z + step) % Z, c) if z // slots_dev == x else None
                    ),
                )
            by_z.append(outgoing)
        by_z = jnp.stack(by_z)
        wanted = (z_at - (x_at * slots_dev + jnp.arange(slots_dev))) % Z
        mine = jnp.take(by_z, wanted, axis=0)
        kept = lax.dynamic_index_in_dim(mine, c_at, 3, keepdims=False)
        given = lax.dynamic_index_in_dim(mine, 1 - c_at, 3, keepdims=False)
        given = send(given, lambda y, x, z, c: (y, x, z, (c + 1) % C))
        both = jnp.where(
            c_at == 0, jnp.stack([kept, given], 2), jnp.stack([given, kept], 2)
        )
        activations = both.transpose(0, 2, 3, 1, 4, 5).reshape(
            slots_dev, Y * X, share, features
        )

        outputs = [None] * LAYERS
        small = [None] * LAYERS
        bias_grads = [None] * LAYERS

        def cut_rows(array, pieces):
            size = array.shape[0] // pieces
            return [array[at * size : (at + 1) * size] for at in range(pieces)]

        def cut_columns(array, pieces):
            size = array.shape[1] // pieces
            return [array[:, at * size : (at + 1) * size] for at in range(pieces)]

        pieces = OWN * Y
        for layer in reversed(range(LAYERS)):
            qkv_full, out_full, up_full, down_full = weights[layer]
            (
                before,
                first_norm,
                mixed,
                log_total,
                context,
                middle,
                second_norm,
                activated,
                act_slope,
            ) = saved[layer]
            gains = norm_gains[layer].astype(F32)
            down_grad = grad_rows.astype(BF16)
            down_bias_grad = jnp.sum(down_grad, 0, dtype=F32)
            down_rows = spread(down_grad)
            up_grad = (dot(down_rows, down_full, 1, 1) * act_slope.astype(F32)).astype(BF16)
            norm_grad = collect(up_grad, up_full, 1)
            grad_down = settle(cut_rows(dot(activated, down_rows, 0, 0), pieces))
            grad_up = settle(cut_columns(dot(second_norm, up_grad, 0, 0), pieces))
            up_bias_grad = jnp.sum(up_grad, 0, dtype=F32)
            added, second_gain, second_shift = norm_back(middle, gains[1], norm_grad)
            grad_rows = grad_rows + added
            attn_grad = grad_rows.astype(BF16)
            out_bias_grad = jnp.sum(attn_grad, 0, dtype=F32)
            attn_rows = spread(attn_grad)
            context_grad = dot(attn_rows, out_full, 1, 1).astype(BF16)
            grad_out = settle(cut_rows(dot(context, attn_rows, 0, 0), pieces))
            mixed_grad = attend_backward(
                *split_heads(mixed),
                slopes,
                position,
                length,
                log_total,
                context_grad.reshape(seq_len, head_here, head_dim),
            ).reshape(seq_len, -1)
            grad_qkv = dot(mixed_grad, first_norm, 0, 0).reshape(3, -1, features)
            grad_qkv = settle(cut_columns(grad_qkv, pieces))
            qkv_bias_grad = jnp.sum(mixed_grad, 0, dtype=F32)
            norm_grad = collect(mixed_grad, qkv_full, 0)
            added, first_gain, first_shift = norm_back(before, gains[0], norm_grad)
            grad_rows = grad_rows + added
            grad_qkv = (
                grad_qkv.transpose(3, 0, 2, 1)
                .reshape(features, shard_heads, head_dim, 3)
                .transpose(0, 1, 3, 2)
                .reshape(features, -1)
            )
            outputs[layer] = (
                grad_qkv.astype(F32),
                grad_out.reshape(-1, features).astype(F32),
                grad_up.transpose(1, 0, 2).reshape(features, -1).astype(F32),
                grad_down.reshape(-1, features).astype(F32),
            )
            small[layer] = jnp.stack(
                [
                    first_gain,
                    second_gain,
                    first_shift,
                    second_shift,
                    out_bias_grad,
                    down_bias_grad,
                ]
            )
            bias_grads[layer] = (qkv_bias_grad.reshape(3, pieces, -1), up_bias_grad)

        bias_pieces = []
        for at in range(pieces):
            row = [bias_grads[layer][0][:, at].reshape(-1) for layer in range(LAYERS)]
            row += [
                bias_grads[layer][1].reshape(pieces, -1)[at] for layer in range(LAYERS)
            ]
            bias_pieces.append(jnp.concatenate(row)[None])
        bias_total = settle(bias_pieces, F32)[:, 0]
        grad_qkv_bias = (
            bias_total[:, :bias_cut]
            .reshape(Y, LAYERS, 3, part_width)
            .transpose(1, 2, 0, 3)
            .reshape(LAYERS, 3, shard_heads, head_dim)
            .transpose(0, 2, 1, 3)
            .reshape(LAYERS, -1)
        )
        grad_up_bias = (
            bias_total[:, bias_cut:].reshape(Y, LAYERS, -1).transpose(1, 0, 2).reshape(LAYERS, -1)
        )

        total = jnp.concatenate(small)
        for size, at in ((C, 3), (X, 1), (Y, 0), (Z, 2)):
            step = 1
            while step < size:
                def flip(*place):
                    place = list(place)
                    place[at] ^= step
                    return tuple(place)

                total = total + send(total, flip)
                step *= 2
        total = total.reshape(LAYERS, 3, 2, features)

        home = (grad_rows * keep_rows).astype(BF16).reshape(blocks, held_len, features)
        input_grad = jnp.zeros((seq_total, held_len, features), BF16)
        at_home = []
        for step in range(Y):
            outgoing = lax.dynamic_index_in_dim(
                home, jnp.clip((y_at + step) % Y - c_at * blocks, 0, blocks - 1), 0, keepdims=False
            )
            if step:
                outgoing = send(
                    outgoing,
                    lambda y, x, z, c: (
                        ((y + step) % Y, x, z, c) if (y + step) % Y // blocks == c else None
                    ),
                )
            at_home.append(outgoing)
        holder = y_at // blocks == c_at
        for step in range(Y):
            mine = at_home[step]
            shared = send(mine, lambda y, x, z, c: ((y, x, z, 1 - c) if y // blocks == c else None))
            mine = jnp.where(holder, mine, shared)
            source_y = (y_at - step) % Y
            half = held_len // C
            half_mine = lax.dynamic_slice_in_dim(mine, c_at * half, half, 0)
            for hop in range(Z):
                source_z = (z_at - hop) % Z
                if hop:
                    part = send(half_mine, lambda y, x, z, c: (y, x, (z + hop) % Z, c))
                    other = send(part, lambda y, x, z, c: (y, x, z, 1 - c))
                    block = jnp.where(
                        c_at == 0,
                        jnp.concatenate([part, other]),
                        jnp.concatenate([other, part]),
                    )
                else:
                    block = mine
                input_grad = lax.dynamic_update_index_in_dim(
                    input_grad, block, seq_deal[source_y * Z + source_z], 0
                )
        return (
            activations,
            input_grad,
            total[:, 0],
            total[:, 1],
            jnp.stack([outputs[layer][0] for layer in range(LAYERS)]),
            grad_qkv_bias,
            jnp.stack([outputs[layer][1] for layer in range(LAYERS)]),
            total[:, 2],
            jnp.stack([outputs[layer][2] for layer in range(LAYERS)]),
            grad_up_bias,
            jnp.stack([outputs[layer][3] for layer in range(LAYERS)]),
        )

    return body


def solution(mesh):
    placed = (
        P(None, "dp", None),
        P(None, "dp", None),
        P(),
        P(),
        P(),
        P(),
        P(None, None, "tensor"),
        P(None, "tensor"),
        P(None, "tensor", None),
        P(),
        P(None, None, "tensor"),
        P(None, "tensor"),
        P(None, "tensor", None),
    )
    return jax.shard_map(
        make_body(mesh.shape["dp"], mesh.shape["tensor"]),
        mesh=mesh,
        in_specs=placed,
        out_specs=(
            P("dp", None, "tensor", None),
            P(None, "dp", None),
            P(),
            P(),
            P(None, None, "tensor"),
            P(None, "tensor"),
            P(None, "tensor", None),
            P(),
            P(None, None, "tensor"),
            P(None, "tensor"),
            P(None, "tensor", None),
        ),
        check_vma=False,
    )
```

```python
import functools
import math

import jax
import jax.numpy as jnp
from jax import lax
from jax.experimental import pallas as pl
from jax.experimental.pallas import tpu as pltpu
from jax.sharding import Mesh
from jax.sharding import PartitionSpec as P

HEADS = 16
LAYERS = 2
EPSILON = 1e-05
BF16 = jnp.bfloat16
F32 = jnp.float32
BIAS_ROWS = 8


def dot(left_side, right_side, left_dim, right_dim):
    return lax.dot_general(
        left_side,
        right_side,
        (((left_dim,), (right_dim,)), ((), ())),
        preferred_element_type=F32,
    )


def norm_parts(values):
    center = values - jnp.mean(values, -1, keepdims=True)
    variance = jnp.mean(center * center, -1, keepdims=True)
    return center, lax.rsqrt(variance + EPSILON)


def layer_norm(values, gain_row, shift_row):
    center, inverse = norm_parts(values)
    return center * inverse * gain_row + shift_row


def norm_back(values, gain_row, norm_grad):
    center, inverse = norm_parts(values)
    unit = center * inverse
    scaled = norm_grad * gain_row
    gain_grad = jnp.sum(norm_grad * unit, 0)
    shift_grad = jnp.sum(norm_grad, 0)
    through = inverse * (
        scaled
        - jnp.mean(scaled, -1, keepdims=True)
        - unit * jnp.mean(scaled * unit, -1, keepdims=True)
    )
    return through, gain_grad, shift_grad


def gelu_pair(values):
    root = math.sqrt(2.0 / math.pi)
    square = values * values
    bend = jnp.tanh(root * values * (1.0 + 0.044715 * square))
    half = 0.5 * (1.0 + bend)
    slope = half + 0.5 * values * (1.0 - bend * bend) * root * (1.0 + 3 * 0.044715 * square)
    return values * half, slope


LOG2E = math.log2(math.e)

def nt(a, b):
    return lax.dot_general(a, b, (((1,), (1,)), ((), ())), preferred_element_type=F32)
def nn(a, b):
    return lax.dot_general(a, b, (((1,), (0,)), ((), ())), preferred_element_type=F32)
def tn(a, b):
    return lax.dot_general(a, b, (((0,), (0,)), ((), ())), preferred_element_type=F32)

def forward_kernel(heads, width, block, places, length, slopes, mixed, context, totals, q_s, k_s, v_s, c_s):
    seq_len = mixed.shape[0]
    count = places.shape[0]
    held = seq_len // count
    span = heads * width
    for at in range(count):
        to = pl.ds(pl.multiple_of(places[at] * held, held), held)
        rows = mixed[at * held:(at + 1) * held, :]
        for head in range(heads):
            q_s[head, to, :] = rows[:, head * width:(head + 1) * width]
            k_s[head, to, :] = rows[:, span + head * width:span + (head + 1) * width]
            v_s[head, to, :] = rows[:, 2 * span + head * width:2 * span + (head + 1) * width]
    limit = length[0]
    row = lax.broadcasted_iota(jnp.int32, (seq_len, 1), 0)
    inside = (lax.broadcasted_iota(jnp.int32, (block, block), 0)
              <= lax.broadcasted_iota(jnp.int32, (block, block), 1))
    scale = LOG2E / math.sqrt(width)
    for head in range(heads):
        bias = jnp.where(row < limit, slopes[head] * LOG2E * row.astype(F32), -1e30)
        for at in range(seq_len // block):
            low, high = at * block, (at + 1) * block
            scores = nt(k_s[head, :high, :], q_s[head, low:high, :]) * scale + bias[:high]
            tail = jnp.where(inside, scores[low:], -1e30)
            scores = jnp.concatenate([scores[:low], tail], 0) if at else tail
            top = jnp.max(scores, 0, keepdims=True)
            probs = jnp.exp2(scores - top)
            total = jnp.sum(probs, 0, keepdims=True)
            probs = (probs * (1.0 / total)).astype(BF16)
            c_s[head, low:high, :] = tn(probs, v_s[head, :high, :]).astype(BF16)
            totals[head:head + 1, low:high] = top + jnp.log2(total)
    for at in range(count):
        frm = pl.ds(pl.multiple_of(places[at] * held, held), held)
        context[at * held:(at + 1) * held, :] = jnp.concatenate([c_s[head, frm, :] for head in range(heads)], 1)

def attend_forward(mixed, places, length, slopes, heads, width):
    seq_len = mixed.shape[0]
    block = min(256, seq_len)
    return pl.pallas_call(
        functools.partial(forward_kernel, heads, width, block),
        out_shape=[jax.ShapeDtypeStruct((seq_len, heads * width), BF16), jax.ShapeDtypeStruct((8, seq_len), F32)],
        in_specs=[pl.BlockSpec(memory_space=pltpu.SMEM)] * 3 + [pl.BlockSpec(memory_space=pltpu.VMEM)],
        out_specs=[pl.BlockSpec(memory_space=pltpu.VMEM)] * 2,
        scratch_shapes=[pltpu.VMEM((heads, seq_len, width), BF16)] * 4,
        compiler_params=pltpu.CompilerParams(vmem_limit_bytes=48 * 2**20),
        cost_estimate=pl.CostEstimate(flops=4 * heads * seq_len * seq_len * width, bytes_accessed=3 * 2**20, transcendentals=heads * seq_len * seq_len // 2),
    )(places, length, slopes, mixed)

def backward_kernel(heads, width, block, places, length, slopes, mixed, context, context_grad, totals, mixed_grad,
                    q_s, k_s, v_s, g_s, dq_s, dk_s, dv_s, stat_s):
    seq_len = mixed.shape[0]
    count = places.shape[0]
    held = seq_len // count
    span = heads * width
    wide = lax.broadcasted_iota(jnp.int32, (held, 128), 1)
    delta_s = stat_s
    for at in range(count):
        to = pl.ds(pl.multiple_of(places[at] * held, held), held)
        rows = mixed[at * held:(at + 1) * held, :]
        grads = context_grad[at * held:(at + 1) * held, :]
        product = grads.astype(F32) * context[at * held:(at + 1) * held, :].astype(F32)
        packed = jnp.zeros((held, 128), F32)
        for head in range(heads):
            q_s[head, to, :] = rows[:, head * width:(head + 1) * width]
            k_s[head, to, :] = rows[:, span + head * width:span + (head + 1) * width]
            v_s[head, to, :] = rows[:, 2 * span + head * width:2 * span + (head + 1) * width]
            g_s[head, to, :] = grads[:, head * width:(head + 1) * width]
            packed = jnp.where(wide == head, jnp.sum(product[:, head * width:(head + 1) * width], 1, keepdims=True), packed)
        delta_s[to, :] = packed
    limit = length[0]
    row = lax.broadcasted_iota(jnp.int32, (seq_len, 1), 0)
    inside = (lax.broadcasted_iota(jnp.int32, (block, block), 0)
              <= lax.broadcasted_iota(jnp.int32, (block, block), 1))
    scale = LOG2E / math.sqrt(width)
    down = 1.0 / math.sqrt(width)
    delta_rows = jnp.transpose(stat_s[...])
    for head in range(heads):
        bias = jnp.where(row < limit, slopes[head] * LOG2E * row.astype(F32), -1e30)
        for at in range(seq_len // block):
            low, high = at * block, (at + 1) * block
            query = q_s[head, low:high, :]
            grads = g_s[head, low:high, :]
            keys = k_s[head, :high, :]
            scores = nt(keys, query) * scale + bias[:high]
            probs = jnp.exp2(scores - totals[head:head + 1, low:high])
            tail = jnp.where(inside, probs[low:], 0.0)
            probs = jnp.concatenate([probs[:low], tail], 0) if at else tail
            low_probs = probs.astype(BF16)
            dprobs = nt(v_s[head, :high, :], grads)
            dscores = (probs * (dprobs - delta_rows[head:head + 1, low:high])).astype(BF16)
            dv = nn(low_probs, grads)
            dk = nn(dscores, query)
            if at:
                dv_s[head, :low, :] += dv[:low]
                dk_s[head, :low, :] += dk[:low]
            dv_s[head, low:high, :] = dv[low:]
            dk_s[head, low:high, :] = dk[low:]
            dq_s[head, low:high, :] = tn(dscores, keys)
    for at in range(count):
        frm = pl.ds(pl.multiple_of(places[at] * held, held), held)
        mixed_grad[at * held:(at + 1) * held, :] = jnp.concatenate(
            [(dq_s[head, frm, :] * down).astype(BF16) for head in range(heads)]
            + [(dk_s[head, frm, :] * down).astype(BF16) for head in range(heads)]
            + [dv_s[head, frm, :].astype(BF16) for head in range(heads)], 1)

def attend_backward(mixed, context, context_grad, totals, places, length, slopes, heads, width):
    seq_len = mixed.shape[0]
    block = min(256, seq_len)
    return pl.pallas_call(
        functools.partial(backward_kernel, heads, width, block),
        out_shape=jax.ShapeDtypeStruct(mixed.shape, BF16),
        in_specs=[pl.BlockSpec(memory_space=pltpu.SMEM)] * 3 + [pl.BlockSpec(memory_space=pltpu.VMEM)] * 4,
        out_specs=pl.BlockSpec(memory_space=pltpu.VMEM),
        scratch_shapes=[pltpu.VMEM((heads, seq_len, width), BF16)] * 4 + [pltpu.VMEM((heads, seq_len, width), F32)] * 3 + [pltpu.VMEM((seq_len, 128), F32)],
        compiler_params=pltpu.CompilerParams(vmem_limit_bytes=48 * 2**20),
        cost_estimate=pl.CostEstimate(flops=10 * heads * seq_len * seq_len * width, bytes_accessed=6 * 2**20, transcendentals=heads * seq_len * seq_len // 2),
    )(places, length, slopes, mixed, context, context_grad, totals)


def make_body(data_size, tensor_size):
    X = math.isqrt(data_size)
    Y = data_size // X
    C = 2
    Z = tensor_size // C
    OWN = Z // X
    AXES = ("y", "x", "z", "c")

    def send(value, rule):
        pairs = []
        for y in range(Y):
            for x in range(X):
                for z in range(Z):
                    for c in range(C):
                        target = rule(y, x, z, c)
                        if target is not None:
                            ty, tx, tz, tc = target
                            pairs.append(
                                (
                                    ((y * X + x) * Z + z) * C + c,
                                    ((ty * X + tx) * Z + tz) * C + tc,
                                )
                            )
        return lax.ppermute(value, AXES, pairs)

    def body(
        tokens,
        cotangent,
        lengths,
        seq_deal,
        norm_gains,
        norm_shifts,
        qkv_weight,
        qkv_bias,
        out_weight,
        proj_bias,
        up_weight,
        up_bias,
        down_weight,
    ):
        y_at, x_at, z_at, c_at = (lax.axis_index(name) for name in ("y", "x", "z", "c"))
        seq_total, held_len, features = tokens.shape
        head_dim = features // HEADS
        group = X * C
        blocks = Y // C
        rows_here = blocks * held_len
        seq_len = rows_here * group
        is_owner = z_at // OWN == x_at

        def spread(rows):
            near = [rows] + [send(rows, lambda y, x, z, c: (y, x, z, (c + 1) % C))]
            pieces = list(near)
            for step in range(1, X):
                got = send(rows, lambda y, x, z, c: (y, (x - step) % X, z, c))
                pieces += [got, send(got, lambda y, x, z, c: (y, x, z, (c + 1) % C))]
            return jnp.concatenate(pieces, 0)

        def collect(left_side, weight, weight_dim):
            half_rows = C * rows_here
            total = None
            for step in list(range(1, X)) + [0]:
                part = dot(
                    left_side[step * half_rows : (step + 1) * half_rows], weight, 1, weight_dim
                ).astype(BF16)
                got = send(part[rows_here:], lambda y, x, z, c: (y, x, z, (c + 1) % C))
                part = part[:rows_here].astype(F32) + got.astype(F32)
                if step:
                    part = send(
                        part.astype(BF16), lambda y, x, z, c: (y, (x + step) % X, z, c)
                    ).astype(F32)
                total = part if total is None else total + part
            return total

        shard_heads = qkv_weight.shape[2] // (3 * head_dim)
        shard_width = shard_heads * head_dim
        cut_by_x = shard_heads % X == 0
        xs = X if cut_by_x else 1
        shards = Z if cut_by_x else OWN
        splits = xs * Y
        part_at = x_at * Y + y_at if cut_by_x else y_at

        def own_part(array, axis):
            size = array.shape[axis] // splits
            return lax.dynamic_slice_in_dim(array, part_at * size, size, axis)

        def fetch(bundle, cuts):
            if cut_by_x:
                got = lax.all_gather(bundle, "z", axis=0)
            else:
                arrived = None
                for step in range(1, Z // OWN):
                    here = send(
                        bundle,
                        lambda y, x, z, c: (
                            (y, x, (z + OWN * step) % Z, c) if z // OWN == x else None
                        ),
                    )
                    arrived = here if arrived is None else arrived + here
                bundle = jnp.where(is_owner, bundle, arrived)
                got = jnp.stack(
                    [bundle]
                    + [
                        send(
                            bundle,
                            lambda y, x, z, c: (y, x, z // OWN * OWN + (z - step) % OWN, c),
                        )
                        for step in range(1, OWN)
                    ]
                )
            results = []
            at = 0
            for cut in cuts:
                piece = got[:, at : at + cut]
                at += cut
                results.append(
                    jnp.stack(
                        [piece]
                        + [
                            send(piece, lambda y, x, z, c: ((y - step) % Y, x, z, c))
                            for step in range(1, Y)
                        ]
                    )
                )
            return results

        def sum_over_y(parts):
            here = parts[0].astype(F32)
            for step in range(1, Y):
                here += send(
                    parts[step].astype(BF16), lambda y, x, z, c: ((y + step) % Y, x, z, c)
                ).astype(F32)
            return here.astype(BF16)

        def settle(sums):
            rows = sums.shape[1]
            if cut_by_x:
                low = lax.psum_scatter(
                    sums.reshape(-1, features), "z", scatter_dimension=0, tiled=True
                )
                full = lax.all_gather(low, ("y", "x"), axis=0)
                return full.reshape(Y, X, rows, features).swapaxes(0, 1).reshape(-1, rows, features)
            here = sums[0].astype(F32)
            for step in range(1, OWN):
                here += send(
                    sums[step],
                    lambda y, x, z, c: (y, x, z // OWN * OWN + (z + step) % OWN, c),
                ).astype(F32)
            low = here.astype(BF16)
            for step in range(1, Z // OWN):
                here += send(
                    low,
                    lambda y, x, z, c: (
                        (y, x, (z + OWN * step) % Z, c)
                        if ((z + OWN * step) % Z) // OWN == x
                        else None
                    ),
                ).astype(F32)
            low = here.astype(BF16)
            arrived = None
            for step in range(1, X):
                got = send(
                    low,
                    lambda y, x, z, c: ((y, (x + step) % X, z, c) if z // OWN == x else None),
                )
                arrived = got if arrived is None else arrived + got
            low = jnp.where(is_owner, low, arrived)
            relative = [low] + [
                send(low, lambda y, x, z, c: ((y - step) % Y, x, z, c)) for step in range(1, Y)
            ]
            return jnp.roll(jnp.stack(relative), y_at, 0)

        part_width = shard_width // splits
        hidden_part = down_weight.shape[1] // splits
        qkv_bias_part = own_part(
            qkv_bias.reshape(LAYERS, shard_heads, 3, head_dim)
            .transpose(0, 2, 1, 3)
            .reshape(LAYERS, 3, shard_width),
            2,
        ).reshape(-1)
        up_bias_part = own_part(up_bias, 1).reshape(-1)
        bias_cut = qkv_bias_part.shape[0]
        bias_size = bias_cut + up_bias_part.shape[0]
        bias_piece = jnp.pad(
            jnp.concatenate([qkv_bias_part, up_bias_part])[None],
            ((0, BIAS_ROWS - 1), (0, features - bias_size)),
        )
        pieces = []
        for layer in range(LAYERS):
            qkv_view = (
                qkv_weight[layer]
                .reshape(features, shard_heads, 3, head_dim)
                .transpose(2, 1, 3, 0)
                .reshape(3, shard_width, features)
            )
            pieces.append(
                (
                    own_part(qkv_view, 1).reshape(-1, features),
                    own_part(out_weight[layer], 0),
                    own_part(up_weight[layer], 1).T,
                    own_part(down_weight[layer], 0),
                )
            )
        weights = []
        for layer in range(LAYERS):
            qkv_piece, out_piece, up_piece, down_piece = pieces[layer]
            if layer == 0:
                with_bias, out_got = fetch(
                    jnp.concatenate([qkv_piece, bias_piece, out_piece]),
                    (3 * part_width + BIAS_ROWS, part_width),
                )
                qkv_got = with_bias[:, :, : 3 * part_width]
                bias_got = with_bias[:, :, 3 * part_width, :bias_size].astype(F32)
                up_got, down_got = fetch(
                    jnp.concatenate([up_piece, down_piece]), (hidden_part, hidden_part)
                )
            else:
                qkv_got, out_got, up_got, down_got = fetch(
                    jnp.concatenate([qkv_piece, out_piece, up_piece, down_piece]),
                    (3 * part_width, part_width, hidden_part, hidden_part),
                )
            weights.append(
                (
                    qkv_got.reshape(Y, shards, 3, part_width, features)
                    .transpose(2, 1, 0, 3, 4)
                    .reshape(-1, features),
                    out_got.swapaxes(0, 1).reshape(-1, features),
                    up_got.reshape(-1, features),
                    down_got.reshape(-1, features),
                )
            )
        full_qkv_bias = (
            bias_got[:, :, :bias_cut]
            .reshape(Y, shards, LAYERS, 3, part_width)
            .transpose(2, 3, 1, 0, 4)
            .reshape(LAYERS, -1)
        )
        full_up_bias = (
            bias_got[:, :, bias_cut:]
            .reshape(Y, shards, LAYERS, hidden_part)
            .transpose(2, 0, 1, 3)
            .reshape(LAYERS, -1)
        )

        head_here = shards * shard_width // (xs * head_dim)
        x_width = shard_width // xs
        element = jnp.arange(head_here) * head_dim
        shard_step = element // x_width
        y_true = (y_at + element % x_width // part_width) % Y
        if cut_by_x:
            shard_z, x_start = shard_step, x_at * x_width
        else:
            shard_z, x_start = x_at * OWN + (z_at + shard_step) % OWN, 0
        column = (shard_z * C + c_at) * shard_width + x_start + y_true * part_width
        slopes = jnp.exp2(-8.0 * (column // head_dim + 1).astype(F32) / HEADS)

        slot = y_at * Z + z_at
        sequence = seq_deal[slot]
        length = lengths[sequence]

        def deal(member):
            pieces = []
            for step in range(Y):
                target = (y_at + step) % Y
                picked = lax.dynamic_index_in_dim(
                    member, seq_deal[target * Z + z_at], 0, keepdims=False
                )
                if step:
                    picked = send(
                        picked,
                        lambda y, x, z, c: (
                            ((y + step) % Y, x, z, c) if y // blocks == c else None
                        ),
                    )
                pieces.append(picked)
            if Y == 2:
                return jnp.where(y_at == c_at, pieces[0], pieces[1])
            stacked = jnp.stack(pieces)
            wanted = (y_at - (c_at * blocks + jnp.arange(blocks))) % Y
            return jnp.take(stacked, wanted, axis=0).reshape(-1, features)

        def positions(x_of, c_of):
            block = (c_of * blocks + jnp.arange(blocks)) * X + x_of
            return (block[:, None] * held_len + jnp.arange(held_len)[None, :]).reshape(-1)

        own_position = positions(x_at, c_at)
        places = jnp.concatenate(
            [
                ((c_at + c_step) % C * blocks + jnp.arange(blocks)) * X + (x_at + x_step) % X
                for x_step in range(X)
                for c_step in range(C)
            ]
        )
        length_row = length[None]
        keep_rows = (own_position < length).astype(F32)[:, None]
        residual = deal(tokens).astype(F32) * keep_rows
        grad_rows = deal(cotangent).astype(F32) * keep_rows

        saved = []
        for layer in range(LAYERS):
            qkv_full, out_full, up_full, down_full = weights[layer]
            gains = norm_gains[layer].astype(F32)
            shifts = norm_shifts[layer].astype(F32)
            biases = proj_bias[layer].astype(F32)
            before = residual
            first_norm = spread(layer_norm(before, gains[0], shifts[0]).astype(BF16))
            mixed = (dot(first_norm, qkv_full, 1, 1) + full_qkv_bias[layer]).astype(BF16)
            context, log_total = attend_forward(
                mixed, places, length_row, slopes, head_here, head_dim
            )
            middle = before + (collect(context, out_full, 0) + biases[0])
            second_norm = spread(layer_norm(middle, gains[1], shifts[1]).astype(BF16))
            upward = dot(second_norm, up_full, 1, 1) + full_up_bias[layer]
            activated, act_slope = gelu_pair(upward)
            activated = activated.astype(BF16)
            act_slope = act_slope.astype(BF16)
            residual = middle + (collect(activated, down_full, 0) + biases[1])
            saved.append(
                (
                    before,
                    first_norm,
                    mixed,
                    log_total,
                    context,
                    middle,
                    second_norm,
                    activated,
                    act_slope,
                )
            )

        final = (residual * keep_rows).astype(BF16)
        slots_dev = seq_total // (Y * X)
        moved = []
        for step in range(X):
            source = final
            if step:
                source = send(
                    final,
                    lambda y, x, z, c: (
                        (y, (x + step) % X, z, c) if (x + step) % X == z // slots_dev else None
                    ),
                )
            moved.append(source)
        moved = jnp.stack(moved)
        order = (x_at - jnp.arange(X)) % X
        moved = jnp.take(moved, order, axis=0)
        share = held_len // tensor_size
        moved = moved.reshape(X, blocks, Z, C, share, features)
        by_z = []
        for step in range(Z):
            outgoing = lax.dynamic_index_in_dim(moved, (z_at + step) % Z, 2, keepdims=False)
            if step:
                outgoing = send(
                    outgoing,
                    lambda y, x, z, c: (
                        (y, x, (z + step) % Z, c) if z // slots_dev == x else None
                    ),
                )
            by_z.append(outgoing)
        by_z = jnp.stack(by_z)
        wanted = (z_at - (x_at * slots_dev + jnp.arange(slots_dev))) % Z
        mine = jnp.take(by_z, wanted, axis=0)
        kept = lax.dynamic_index_in_dim(mine, c_at, 3, keepdims=False)
        given = lax.dynamic_index_in_dim(mine, 1 - c_at, 3, keepdims=False)
        given = send(given, lambda y, x, z, c: (y, x, z, (c + 1) % C))
        both = jnp.where(
            c_at == 0, jnp.stack([kept, given], 2), jnp.stack([given, kept], 2)
        )
        activations = both.transpose(0, 2, 3, 1, 4, 5).reshape(
            slots_dev, Y * X, share, features
        )

        outputs = [None] * LAYERS
        small = [None] * LAYERS
        bias_grads = [None] * LAYERS

        def hidden_grad(left_side, right_side):
            size = left_side.shape[1] // Y
            return sum_over_y(
                [
                    dot(left_side[:, at * size : (at + 1) * size], right_side, 0, 0).reshape(
                        shards, hidden_part, features
                    )
                    for at in range(Y)
                ]
            )

        for layer in reversed(range(LAYERS)):
            qkv_full, out_full, up_full, down_full = weights[layer]
            (
                before,
                first_norm,
                mixed,
                log_total,
                context,
                middle,
                second_norm,
                activated,
                act_slope,
            ) = saved[layer]
            gains = norm_gains[layer].astype(F32)
            down_grad = grad_rows.astype(BF16)
            down_bias_grad = jnp.sum(down_grad, 0, dtype=F32)
            down_rows = spread(down_grad)
            up_grad = (dot(down_rows, down_full, 1, 1) * act_slope.astype(F32)).astype(BF16)
            norm_grad = collect(up_grad, up_full, 0)
            hidden = settle(
                jnp.concatenate(
                    [hidden_grad(activated, down_rows), hidden_grad(up_grad, second_norm)], 1
                )
            )
            up_bias_grad = jnp.sum(up_grad, 0, dtype=F32)
            added, second_gain, second_shift = norm_back(middle, gains[1], norm_grad)
            grad_rows = grad_rows + added
            attn_grad = grad_rows.astype(BF16)
            out_bias_grad = jnp.sum(attn_grad, 0, dtype=F32)
            attn_rows = spread(attn_grad)
            context_grad = dot(attn_rows, out_full, 1, 1).astype(BF16)
            grad_out = dot(context, attn_rows, 0, 0).astype(BF16)
            mixed_grad = attend_backward(
                mixed,
                context,
                context_grad,
                log_total,
                places,
                length_row,
                slopes,
                head_here,
                head_dim,
            )
            grad_qkv = dot(mixed_grad, first_norm, 0, 0).astype(BF16)
            qkv_bias_grad = jnp.sum(mixed_grad, 0, dtype=F32)
            bias_grads[layer] = (
                qkv_bias_grad.reshape(3, shards, Y, part_width)
                .transpose(2, 1, 0, 3)
                .reshape(Y, shards, -1),
                up_bias_grad.reshape(Y, shards, -1),
            )
            parts = [
                grad_out.reshape(shards, Y, part_width, features).swapaxes(0, 1),
                grad_qkv.reshape(3, shards, Y, part_width, features)
                .transpose(2, 1, 0, 3, 4)
                .reshape(Y, shards, -1, features),
            ]
            if layer == 0:
                bias_row = jnp.concatenate(
                    [entry[0] for entry in bias_grads] + [entry[1] for entry in bias_grads], 2
                ).astype(BF16)
                parts.append(
                    jnp.pad(
                        bias_row[:, :, None],
                        ((0, 0), (0, 0), (0, BIAS_ROWS - 1), (0, features - bias_size)),
                    )
                )
            parts = jnp.concatenate(parts, 2)
            attention = settle(sum_over_y(parts))
            norm_grad = collect(mixed_grad, qkv_full, 0)
            added, first_gain, first_shift = norm_back(before, gains[0], norm_grad)
            grad_rows = grad_rows + added
            grad_qkv = (
                attention[:, part_width : 4 * part_width]
                .reshape(splits, 3, part_width, features)
                .transpose(3, 0, 2, 1)
                .reshape(features, shard_heads, head_dim, 3)
                .transpose(0, 1, 3, 2)
                .reshape(features, -1)
            )
            outputs[layer] = (
                grad_qkv.astype(F32),
                attention[:, :part_width].reshape(-1, features).astype(F32),
                hidden[:, hidden_part:].reshape(-1, features).T.astype(F32),
                hidden[:, :hidden_part].reshape(-1, features).astype(F32),
            )
            small[layer] = jnp.stack(
                [
                    first_gain,
                    second_gain,
                    first_shift,
                    second_shift,
                    out_bias_grad,
                    down_bias_grad,
                ]
            )
        bias_total = attention[:, 4 * part_width, :bias_size].astype(F32)
        grad_qkv_bias = (
            bias_total[:, :bias_cut]
            .reshape(splits, LAYERS, 3, part_width)
            .transpose(1, 2, 0, 3)
            .reshape(LAYERS, 3, shard_heads, head_dim)
            .transpose(0, 2, 1, 3)
            .reshape(LAYERS, -1)
        )
        grad_up_bias = (
            bias_total[:, bias_cut:]
            .reshape(splits, LAYERS, -1)
            .transpose(1, 0, 2)
            .reshape(LAYERS, -1)
        )

        total = jnp.concatenate(small)
        for size, at in ((C, 3), (X, 1), (Y, 0), (Z, 2)):
            step = 1
            while step < size:
                def flip(*place):
                    place = list(place)
                    place[at] ^= step
                    return tuple(place)

                total = total + send(total, flip)
                step *= 2
        total = total.reshape(LAYERS, 3, 2, features)

        home = (grad_rows * keep_rows).astype(BF16).reshape(blocks, held_len, features)
        input_grad = jnp.zeros((seq_total, held_len, features), BF16)
        at_home = []
        for step in range(Y):
            outgoing = lax.dynamic_index_in_dim(
                home, jnp.clip((y_at + step) % Y - c_at * blocks, 0, blocks - 1), 0, keepdims=False
            )
            if step:
                outgoing = send(
                    outgoing,
                    lambda y, x, z, c: (
                        ((y + step) % Y, x, z, c) if (y + step) % Y // blocks == c else None
                    ),
                )
            at_home.append(outgoing)
        holder = y_at // blocks == c_at
        for step in range(Y):
            mine = at_home[step]
            shared = send(mine, lambda y, x, z, c: ((y, x, z, 1 - c) if y // blocks == c else None))
            mine = jnp.where(holder, mine, shared)
            source_y = (y_at - step) % Y
            half = held_len // C
            half_mine = lax.dynamic_slice_in_dim(mine, c_at * half, half, 0)
            for hop in range(Z):
                source_z = (z_at - hop) % Z
                if hop:
                    part = send(half_mine, lambda y, x, z, c: (y, x, (z + hop) % Z, c))
                    other = send(part, lambda y, x, z, c: (y, x, z, 1 - c))
                    block = jnp.where(
                        c_at == 0,
                        jnp.concatenate([part, other]),
                        jnp.concatenate([other, part]),
                    )
                else:
                    block = mine
                input_grad = lax.dynamic_update_index_in_dim(
                    input_grad, block, seq_deal[source_y * Z + source_z], 0
                )
        return (
            activations,
            input_grad,
            total[:, 0],
            total[:, 1],
            jnp.stack([outputs[layer][0] for layer in range(LAYERS)]),
            grad_qkv_bias,
            jnp.stack([outputs[layer][1] for layer in range(LAYERS)]),
            total[:, 2],
            jnp.stack([outputs[layer][2] for layer in range(LAYERS)]),
            grad_up_bias,
            jnp.stack([outputs[layer][3] for layer in range(LAYERS)]),
        )

    return body


def solution(mesh):
    data_size, tensor_size = mesh.shape["dp"], mesh.shape["tensor"]
    x_size = math.isqrt(data_size)
    fine = Mesh(
        mesh.devices.reshape(data_size // x_size, x_size, tensor_size // 2, 2),
        ("y", "x", "z", "c"),
    )
    data, tensor = ("y", "x"), ("z", "c")
    placed = (
        P(None, data, None),
        P(None, data, None),
        P(),
        P(),
        P(),
        P(),
        P(None, None, tensor),
        P(None, tensor),
        P(None, tensor, None),
        P(),
        P(None, None, tensor),
        P(None, tensor),
        P(None, tensor, None),
    )
    return jax.shard_map(
        make_body(data_size, tensor_size),
        mesh=fine,
        in_specs=placed,
        out_specs=(
            P(data, None, tensor, None),
            P(None, data, None),
            P(),
            P(),
            P(None, None, tensor),
            P(None, tensor),
            P(None, tensor, None),
            P(),
            P(None, None, tensor),
            P(None, tensor),
            P(None, tensor, None),
        ),
        check_vma=False,
    )
```
